32 devices in a mesh: ctx: 8 (over z, y), head: 4 (over x, core).
Axes of the slice: x: 2, y: 2, z: 4, core: 2. Of those that a mesh axis runs over, the one named last changes fastest.
Arguments:
- tokens: bfloat16 [1024, 2048], P('ctx'), may hold values from -6 to 6
- grad_out: bfloat16 [1024, 2048], P('ctx'), may hold values from -6 to 6
- expert_ids: int32 [1024, 8], P('ctx'), may hold values from 0 to 15, all different within a row; in each aligned block of 128 rows (0 to 127, 128 to 255, ...) at most 80 rows name the same one
- gate_probs: bfloat16 [1024, 8], P('ctx'), may hold values from 0.029907227 to 0.3984375
- w_gate: bfloat16 [16, 768, 2048], P('ctx', 'head'), may hold values from -0.125 to 0.125
- w_up: bfloat16 [16, 768, 2048], P('ctx', 'head'), may hold values from -0.125 to 0.125
- w_down: bfloat16 [16, 768, 2048], P('ctx', 'head'), may hold values from -0.21875 to 0.21875
- query_rows: bfloat16 [1024, 4096], P('ctx', 'head'), may hold values from -4.5 to 4.5, as said below
- key_rows: bfloat16 [1024, 512], P('ctx', 'head'), may hold values from -4.5 to 4.5, as said below
- value_rows: bfloat16 [1024, 512], P('ctx', 'head'), may hold values from -6 to 6
- attn_out: bfloat16 [1024, 4096], P('ctx', 'head'), may hold values from -6 to 6
- grad_attn: bfloat16 [1024, 4096], P('ctx', 'head'), may hold values from -6 to 6
- segment_ids: int32 [1024], replicated, may hold values from 0 to 7, never falling along the last dimension, each value on 1 to 384 neighbouring positions
Outputs:
- grad_tokens: bfloat16 [1024, 2048], P('ctx')
- grad_gate: bfloat16 [16, 768, 2048], P('ctx', 'head')
- grad_up: bfloat16 [16, 768, 2048], P('ctx', 'head')
- grad_down: bfloat16 [16, 768, 2048], P('ctx', 'head')
- grad_query: bfloat16 [1024, 4096], P('ctx', 'head')
- grad_key: bfloat16 [1024, 512], P('ctx', 'head')
- grad_value: bfloat16 [1024, 512], P('ctx', 'head')
The draws below stay inside these ranges and needn't reach their ends.
Inputs may be any that keep to these rules, and one draw needn't show every extreme that they name: `expert_ids`: each row names different experts; among the 128 tokens of one index of ctx no expert is named more than 80 times, a bound that some block reaches. `segment_ids`: ids never fall; a document has at most 384 positions, and one has exactly that many. `query_rows`: entries stay within the range. `key_rows`: entries stay within the range.
All inputs are finite; a program needn't handle non-finite values.
Results may differ from the reference program's by a relative error of at most 0.0057.
Values may be sent and summed in bfloat16 or wider, within the bound.
A program may use at most 128 MiB of HBM per device.

```python
import math
import jax
import jax.numpy as jnp
import numpy as np
from jax import lax

D = 2048
FF = 768
TOPK = 8
HQ = 32
KVH = 4
HD = 128
TOK_DEV = 128
ATT_DEV = 128
REACH = 3
EXPERTS = 16
CAP = 80
TOKENS = 1024
ATT_TOK = 1024
N_CTX = 8


def drawn_pair(base_key):
    folded = jax.random.fold_in(base_key, 4242)
    subkeys = jax.random.split(folded, 2)
    query_draw = jnp.clip(jax.random.normal(subkeys[0], (ATT_TOK, HQ * HD), jnp.float32), -4.5, 4.5)
    key_draw = jnp.clip(jax.random.normal(subkeys[1], (ATT_TOK, KVH * HD), jnp.float32), -4.5, 4.5)
    return (query_draw, key_draw)


def draw_query_rows(key, part):
    return drawn_pair(key)[0].astype(jnp.bfloat16)


def draw_key_rows(key, part):
    return drawn_pair(key)[1].astype(jnp.bfloat16)


def levels(key, dims, shards, low, top_value):
    gain, own = 1.0, jax.random.fold_in(key, 6)
    for axis_at, blocks in shards:
        heights = jnp.exp(jax.random.uniform(jax.random.fold_in(own, axis_at), (blocks,), jnp.float32, low / len(shards), top_value / len(shards)))
        gain = gain * jnp.repeat(heights, dims[axis_at] // blocks).reshape([-1 if axis == axis_at else 1 for axis in range(len(dims))])
    return gain


def profile(count, total, most, lean):
    portions = [(1 << 20) // math.isqrt(grade ** lean) + 1 for grade in range(2, count + 1)]
    surplus, counts = total - most - (count - 1), [1] * (count - 1)
    while surplus > 0:
        movable = [i for i in range(count - 1) if counts[i] < most]
        mass, remaining = sum([portions[i] for i in movable]), surplus
        for i in movable:
            more = min(most - counts[i], max(1, remaining * portions[i] // mass), surplus)
            counts[i] = counts[i] + more
            surplus = surplus - more
    return np.array([most] + counts)


def uneven_parts(own_key, number_of, total, most, lean):
    if number_of == 2:
        one = jax.random.randint(own_key, (), max(1, total - most), min(most, total - 1) + 1)
        return jnp.stack([one, total - one])
    lengths = jnp.asarray(profile(number_of, total, most, lean), jnp.int32)
    couples = (number_of - 1) // 2
    donor, receiver = lengths[1:1 + 2 * couples:2], lengths[2:2 + 2 * couples:2]
    margin = jnp.minimum(donor - 1, most - receiver)
    passed = jax.random.randint(jax.random.fold_in(own_key, 1), (couples,), 0, 1 << 20) % (margin + 1)
    lengths = lengths.at[1:1 + 2 * couples:2].set(donor - passed).at[2:2 + 2 * couples:2].set(receiver + passed)
    return lengths[jax.random.permutation(jax.random.fold_in(own_key, 2), number_of)]


def assign_block(stream_key, own, number, rows, amount, top, bound, lean):
    ranking = jax.random.permutation(stream_key, amount)
    heavy_load, usual = shares(amount, rows * top, bound, lean, True), shares(amount, rows * top, bound, lean, False)
    places = jnp.arange(amount)

    def named(lengths, turn):
        used = int((lengths > 0).sum())
        fixed = max(1, used // 4)
        passed = fixed + (places - fixed + turn * (used - fixed)) % max(1, amount - fixed)
        return jnp.zeros((amount,), jnp.int32).at[ranking[jnp.where(places < fixed, places, passed)]].set(jnp.asarray(lengths, jnp.int32))

    lengths = jnp.where(number % 4 == 0, named(heavy_load, number // 4), named(usual, number - number // 4 - 1))
    mixed = jax.random.permutation(jax.random.fold_in(own, 3), amount)
    source_of, receiver = mixed[0:amount // 2 * 2:2], mixed[1:amount // 2 * 2:2]
    margin = jnp.minimum(lengths[source_of] - 1, bound - lengths[receiver]) // 2
    margin = jnp.where((source_of == ranking[0]) | (receiver == ranking[0]) | (lengths[receiver] == 0), 0, jnp.maximum(margin, 0))
    passed = jax.random.randint(jax.random.fold_in(own, 4), (amount // 2,), 0, 1 << 20) % (margin + 1)
    lengths = lengths.at[source_of].add(-passed).at[receiver].add(passed)
    members = jnp.searchsorted(jnp.cumsum(lengths), jnp.arange(rows * top), side="right").astype(jnp.int32)
    table = members.reshape(top, rows).T
    table = table[jax.random.permutation(jax.random.fold_in(own, 1), rows)]
    turn = jax.random.randint(jax.random.fold_in(own, 2), (rows, 1), 0, top)
    return jnp.take_along_axis(table, (jnp.arange(top)[None, :] + turn) % top, axis=1)


def shares(number_of, total, most, lean, full):
    loads = [(1 << 20) // math.isqrt(grade ** lean) + 1 for grade in range(1, number_of + 1)]
    largest = most if full else min(most, max(-(-total // number_of), total * loads[0] // sum(loads)))
    least = 1 if total - largest >= number_of - 1 else 0
    holding, surplus = [largest] + [least] * (number_of - 1), total - largest - least * (number_of - 1)
    while surplus > 0:
        candidates = [i for i in range(1, number_of) if holding[i] < largest] or [i for i in range(1, number_of) if holding[i] < most]
        whole, left = sum([loads[i] for i in candidates]), surplus
        for i in candidates:
            extra = min(most - holding[i], max(1, left * loads[i] // whole), surplus)
            holding[i] = holding[i] + extra
            surplus = surplus - extra
    return np.array(holding)


def gaussian(rng, dims, scale, bound, cuts=(), kind=jnp.bfloat16):
    factor_of = levels(rng, dims, cuts, -0.22, 0.18) if cuts else 1.0
    values = jax.random.normal(rng, dims, jnp.float32) * scale * factor_of
    return jnp.minimum(jnp.maximum(values, -bound), bound).astype(kind)


def setup_inputs(seed: int = 0) -> dict:
    arg_keys = jax.random.split(jax.random.key(seed), 14)
    tokens = gaussian(arg_keys[0], (TOKENS, D), 1.0, 6.0, ((0, 8),))
    grad_out = gaussian(arg_keys[1], (TOKENS, D), 1.0, 6.0, ((0, 8),))
    expert_ids_keys = jax.random.split(jax.random.fold_in(arg_keys[2], 1), TOKENS // TOK_DEV)
    expert_ids_turns = jax.random.permutation(jax.random.fold_in(arg_keys[2], 3), TOKENS // TOK_DEV)
    expert_ids = jax.vmap(lambda own, number: assign_block(jax.random.fold_in(arg_keys[2], 2), own, number, TOK_DEV, EXPERTS, TOPK, CAP, 2))(expert_ids_keys, expert_ids_turns).reshape((TOKENS, TOPK))
    gate_probs = jnp.clip(jnp.exp(math.log(0.3984375) - 2.5894505 * jax.random.uniform(arg_keys[3], (TOKENS, TOPK), jnp.float32) ** levels(arg_keys[3], (TOKENS, TOPK), ((0, 8),), -0.2, 0.2)), 0.029907227, 0.3984375).astype(jnp.bfloat16)
    w_gate = gaussian(arg_keys[4], (EXPERTS, FF, D), D ** -0.5, 0.125, ((0, 8), (1, 4)))
    w_up = gaussian(arg_keys[5], (EXPERTS, FF, D), D ** -0.5, 0.125, ((0, 8), (1, 4)))
    w_down = gaussian(arg_keys[6], (EXPERTS, FF, D), FF ** -0.5, 0.21875, ((0, 8), (1, 4)))
    query_rows = draw_query_rows(jax.random.fold_in(arg_keys[13], 71), 0)
    key_rows = draw_key_rows(jax.random.fold_in(arg_keys[13], 71), 0)
    value_rows = gaussian(arg_keys[9], (ATT_TOK, KVH * HD), 1.0, 6.0, ((0, 8), (1, 4)))
    attn_out = gaussian(arg_keys[10], (ATT_TOK, HQ * HD), 1.0, 6.0, ((0, 8), (1, 4)))
    grad_attn = gaussian(arg_keys[11], (ATT_TOK, HQ * HD), 1.0, 6.0, ((0, 8), (1, 4)))
    segment_ids = jnp.searchsorted(jnp.cumsum(uneven_parts(arg_keys[12], N_CTX, ATT_TOK, REACH * ATT_DEV, 2)), jnp.arange(ATT_TOK), side="right").astype(jnp.int32)
    return dict(tokens=tokens, grad_out=grad_out, expert_ids=expert_ids, gate_probs=gate_probs, w_gate=w_gate, w_up=w_up, w_down=w_down, query_rows=query_rows, key_rows=key_rows, value_rows=value_rows, attn_out=attn_out, grad_attn=grad_attn, segment_ids=segment_ids)


def expert_terms(rows_in, grad_rows, gate_mat, up_mat, down_mat):
    gate_pre = jnp.dot(rows_in, gate_mat.T, preferred_element_type=jnp.float32)
    up_pre = jnp.dot(rows_in, up_mat.T, preferred_element_type=jnp.float32)
    sigmoid_gate = jax.nn.sigmoid(gate_pre)
    active = gate_pre * sigmoid_gate
    hidden = (active * up_pre).astype(jnp.bfloat16)
    hidden_grad = jnp.dot(grad_rows, down_mat.T, preferred_element_type=jnp.float32)
    gate_grad = (hidden_grad * up_pre * sigmoid_gate * (1.0 + gate_pre * (1.0 - sigmoid_gate))).astype(jnp.bfloat16)
    up_grad = (hidden_grad * active).astype(jnp.bfloat16)
    returned = jnp.dot(gate_grad, gate_mat, preferred_element_type=jnp.float32) + jnp.dot(up_grad, up_mat, preferred_element_type=jnp.float32)
    gate_part = jnp.dot(gate_grad.T, rows_in, preferred_element_type=jnp.float32).astype(jnp.bfloat16)
    up_part = jnp.dot(up_grad.T, rows_in, preferred_element_type=jnp.float32).astype(jnp.bfloat16)
    down_part = jnp.dot(hidden.T, grad_rows, preferred_element_type=jnp.float32).astype(jnp.bfloat16)
    return returned, gate_part, up_part, down_part


def moe_backward(tokens, grad_out, expert_ids, gate_probs, w_gate, w_up, w_down):
    pair_count = TOKENS * TOPK
    slot_total = N_CTX * CAP
    flat_expert = expert_ids.reshape(pair_count)
    padded_tokens = jnp.concatenate([tokens, jnp.zeros((1, D), tokens.dtype)], axis=0)
    padded_grad = jnp.concatenate([grad_out, jnp.zeros((1, D), grad_out.dtype)], axis=0)
    padded_probs = jnp.concatenate([gate_probs.reshape(pair_count).astype(jnp.float32), jnp.zeros((1,), jnp.float32)])

    def expert_step(accumulated, expert):
        pair_list = jnp.nonzero(flat_expert == expert, size=slot_total, fill_value=pair_count)[0].astype(jnp.int32)
        token_list = (pair_list // TOPK).astype(jnp.int32)
        rows_in = padded_tokens[token_list]
        grad_rows = (padded_probs[pair_list][:, None] * padded_grad[token_list].astype(jnp.float32)).astype(jnp.bfloat16)
        returned, gate_part, up_part, down_part = expert_terms(rows_in, grad_rows, w_gate[expert], w_up[expert], w_down[expert])
        accumulated = accumulated.at[token_list].add(returned)
        return accumulated, (gate_part, up_part, down_part)

    start_sum = jnp.zeros((TOKENS + 1, D), jnp.float32)
    summed, grads = lax.scan(expert_step, start_sum, jnp.arange(EXPERTS, dtype=jnp.int32))
    return summed[:TOKENS].astype(jnp.bfloat16), grads[0], grads[1], grads[2]


def attention_backward(query_rows, key_rows, value_rows, attn_out, grad_attn, segment_ids):
    group_size = HQ // KVH
    window = (REACH + 1) * ATT_DEV
    pad_rows = REACH * ATT_DEV
    score_scale = HD ** -0.5
    padded_key = jnp.concatenate([jnp.zeros((pad_rows, KVH * HD), key_rows.dtype), key_rows], axis=0)
    padded_value = jnp.concatenate([jnp.zeros((pad_rows, KVH * HD), value_rows.dtype), value_rows], axis=0)
    padded_segment = jnp.concatenate([jnp.full((pad_rows,), -1, jnp.int32), segment_ids.astype(jnp.int32)])
    positions = jnp.arange(ATT_TOK + pad_rows, dtype=jnp.int32) - pad_rows

    def block_step(carried, block_index):
        key_accum, value_accum = carried
        row_start = (block_index * ATT_DEV).astype(jnp.int32)
        query_heads = lax.dynamic_slice_in_dim(query_rows, row_start, ATT_DEV, 0).astype(jnp.float32).reshape(ATT_DEV, KVH, group_size, HD)
        out_heads = lax.dynamic_slice_in_dim(attn_out, row_start, ATT_DEV, 0).astype(jnp.float32).reshape(ATT_DEV, KVH, group_size, HD)
        grad_heads = lax.dynamic_slice_in_dim(grad_attn, row_start, ATT_DEV, 0).astype(jnp.float32).reshape(ATT_DEV, KVH, group_size, HD)
        window_key = lax.dynamic_slice_in_dim(padded_key, row_start, window, 0).astype(jnp.float32).reshape(window, KVH, HD)
        window_value = lax.dynamic_slice_in_dim(padded_value, row_start, window, 0).astype(jnp.float32).reshape(window, KVH, HD)
        query_pos = row_start + jnp.arange(ATT_DEV, dtype=jnp.int32)
        key_pos = lax.dynamic_slice_in_dim(positions, row_start, window, 0)
        query_seg = lax.dynamic_slice_in_dim(segment_ids.astype(jnp.int32), row_start, ATT_DEV, 0)
        key_seg = lax.dynamic_slice_in_dim(padded_segment, row_start, window, 0)
        visible = (key_pos[None, :] <= query_pos[:, None]) & (key_seg[None, :] == query_seg[:, None])
        scores = jnp.einsum("ajgd,tjd->jgat", query_heads, window_key) * score_scale
        row_peak = jnp.max(jnp.where(visible, scores, -jnp.inf), axis=-1, keepdims=True)
        weights_exp = jnp.exp(jnp.where(visible, scores - row_peak, -jnp.inf))
        probs = weights_exp / jnp.sum(weights_exp, axis=-1, keepdims=True)
        row_delta = jnp.einsum("ajgd,ajgd->jga", grad_heads, out_heads)
        prob_grad = jnp.einsum("ajgd,tjd->jgat", grad_heads, window_value)
        score_grad = (probs * (prob_grad - row_delta[..., None])).astype(jnp.bfloat16)
        probs_low = probs.astype(jnp.bfloat16)
        grad_query = (score_scale * jnp.einsum("jgat,tjd->ajgd", score_grad.astype(jnp.float32), window_key)).astype(jnp.bfloat16)
        key_terms = (score_scale * jnp.einsum("jgat,ajgd->tjd", score_grad.astype(jnp.float32), query_heads)).reshape(window, KVH * HD)
        value_terms = jnp.einsum("jgat,ajgd->tjd", probs_low.astype(jnp.float32), grad_heads).reshape(window, KVH * HD)
        key_accum = lax.dynamic_update_slice_in_dim(key_accum, lax.dynamic_slice_in_dim(key_accum, row_start, window, 0) + key_terms, row_start, 0)
        value_accum = lax.dynamic_update_slice_in_dim(value_accum, lax.dynamic_slice_in_dim(value_accum, row_start, window, 0) + value_terms, row_start, 0)
        return (key_accum, value_accum), grad_query.reshape(ATT_DEV, HQ * HD)

    start_key = jnp.zeros((ATT_TOK + pad_rows, KVH * HD), jnp.float32)
    start_value = jnp.zeros((ATT_TOK + pad_rows, KVH * HD), jnp.float32)
    carried, blocks = lax.scan(block_step, (start_key, start_value), jnp.arange(N_CTX, dtype=jnp.int32))
    grad_query = blocks.reshape(ATT_TOK, HQ * HD)
    return grad_query, carried[0][pad_rows:].astype(jnp.bfloat16), carried[1][pad_rows:].astype(jnp.bfloat16)


def reference(tokens, grad_out, expert_ids, gate_probs, w_gate, w_up, w_down, query_rows, key_rows, value_rows, attn_out, grad_attn, segment_ids):
    grad_tokens, grad_gate, grad_up, grad_down = moe_backward(tokens, grad_out, expert_ids, gate_probs, w_gate, w_up, w_down)
    grad_query, grad_key, grad_value = attention_backward(query_rows, key_rows, value_rows, attn_out, grad_attn, segment_ids)
    return (grad_tokens, grad_gate, grad_up, grad_down, grad_query, grad_key, grad_value)
```

```python
import jax
import jax.numpy as jnp
from jax import lax
from jax.sharding import PartitionSpec as P

HQ = 32
KVH = 4
HD = 128
REACH = 3


def passed_along(block, axis, distance):
    devices = range(lax.axis_size(axis))
    route = [(i - distance, i) for i in devices if i - distance in devices]
    return lax.ppermute(block, axis, route)


def expert_backward(recv_rows, recv_grads, w_gate, w_up, w_down):
    gate_pre = jnp.einsum("secd,efd->secf", recv_rows, w_gate, preferred_element_type=jnp.float32)
    up_pre = jnp.einsum("secd,efd->secf", recv_rows, w_up, preferred_element_type=jnp.float32)
    sigmoid_gate = jax.nn.sigmoid(gate_pre)
    active = gate_pre * sigmoid_gate
    hidden = (active * up_pre).astype(jnp.bfloat16)
    hidden_grad = jnp.einsum(
        "secd,efd->secf", recv_grads, w_down, preferred_element_type=jnp.float32
    )
    gate_grad = (
        hidden_grad * up_pre * sigmoid_gate * (1.0 + gate_pre * (1.0 - sigmoid_gate))
    ).astype(jnp.bfloat16)
    up_grad = (hidden_grad * active).astype(jnp.bfloat16)
    back_rows = jnp.einsum(
        "secf,efd->secd", gate_grad, w_gate, preferred_element_type=jnp.float32
    ) + jnp.einsum("secf,efd->secd", up_grad, w_up, preferred_element_type=jnp.float32)
    grad_gate = jnp.einsum(
        "secf,secd->efd", gate_grad, recv_rows, preferred_element_type=jnp.float32
    ).astype(jnp.bfloat16)
    grad_up = jnp.einsum(
        "secf,secd->efd", up_grad, recv_rows, preferred_element_type=jnp.float32
    ).astype(jnp.bfloat16)
    grad_down = jnp.einsum(
        "secf,secd->efd", hidden, recv_grads, preferred_element_type=jnp.float32
    ).astype(jnp.bfloat16)
    return (back_rows, grad_gate, grad_up, grad_down)


def pair_total(returned, slot_index, tok_count, top_count):
    flat_rows = returned.reshape(-1, returned.shape[3])
    picked = flat_rows[slot_index]
    return jnp.sum(picked.reshape(tok_count, top_count, returned.shape[3]), axis=1)


def routed_experts(tokens, grad_out, expert_ids, gate_probs, w_gate, w_up, w_down):
    tok_count, width = tokens.shape
    top_count = expert_ids.shape[1]
    ctx_count = lax.axis_size("ctx")
    local_experts = w_gate.shape[0]
    total_experts = local_experts * ctx_count
    capacity = (5 * tok_count * top_count + 4 * total_experts - 1) // (4 * total_experts)
    pair_count = tok_count * top_count
    flat_expert = expert_ids.reshape(pair_count)
    onehot = (flat_expert[:, None] == jnp.arange(total_experts, dtype=jnp.int32)[None, :]).astype(
        jnp.int32
    )
    earlier = jnp.cumsum(onehot, axis=0) - onehot
    slot_rank = jnp.sum(earlier * onehot, axis=1)
    slot_index = flat_expert * capacity + slot_rank
    slot_pair = (
        jnp.full((total_experts * capacity,), pair_count, jnp.int32)
        .at[slot_index]
        .set(jnp.arange(pair_count, dtype=jnp.int32))
    )
    slot_token = slot_pair // top_count
    padded_tokens = jnp.concatenate([tokens, jnp.zeros((1, width), tokens.dtype)], axis=0)
    padded_grad = jnp.concatenate([grad_out, jnp.zeros((1, width), grad_out.dtype)], axis=0)
    padded_probs = jnp.concatenate(
        [gate_probs.reshape(pair_count).astype(jnp.float32), jnp.zeros((1,), jnp.float32)]
    )
    buffer_shape = (ctx_count, local_experts, capacity, width)
    send_rows = padded_tokens[slot_token].reshape(buffer_shape)
    send_grads = (
        (padded_probs[slot_pair][:, None] * padded_grad[slot_token].astype(jnp.float32))
        .astype(jnp.bfloat16)
        .reshape(buffer_shape)
    )
    recv_rows, recv_grads = (
        lax.all_to_all(send_rows, "ctx", split_axis=0, concat_axis=0, tiled=True),
        lax.all_to_all(send_grads, "ctx", split_axis=0, concat_axis=0, tiled=True),
    )
    back_rows, grad_gate, grad_up, grad_down = expert_backward(
        recv_rows, recv_grads, w_gate, w_up, w_down
    )
    shared = lax.psum_scatter(back_rows, "head", scatter_dimension=3, tiled=True)
    returned = lax.all_to_all(shared, "ctx", split_axis=0, concat_axis=0, tiled=True)
    summed = pair_total(returned, slot_index, tok_count, top_count)
    grad_tokens = lax.all_gather(summed.astype(jnp.bfloat16), "head", axis=1, tiled=True)
    return grad_tokens, grad_gate, grad_up, grad_down


def dense_experts(tokens, grad_out, expert_ids, gate_probs, w_gate, w_up, w_down):
    ctx_count = lax.axis_size("ctx")
    local_experts = w_gate.shape[0]
    total_experts = local_experts * ctx_count
    chosen = expert_ids[:, :, None] == jnp.arange(total_experts, dtype=jnp.int32)[None, None, :]
    prob_table = jnp.sum(
        jnp.where(chosen, gate_probs.astype(jnp.float32)[:, :, None], 0.0), axis=1
    )
    all_tokens = lax.all_gather(tokens, "ctx", axis=0, tiled=True)
    all_grads = lax.all_gather(grad_out, "ctx", axis=0, tiled=True)
    all_probs = lax.all_gather(prob_table, "ctx", axis=0, tiled=True)
    my_probs = lax.dynamic_slice_in_dim(
        all_probs, lax.axis_index("ctx") * local_experts, local_experts, 1
    )
    pair_grads = (my_probs.T[:, :, None] * all_grads.astype(jnp.float32)[None]).astype(jnp.bfloat16)
    gate_pre = jnp.einsum("td,efd->etf", all_tokens, w_gate, preferred_element_type=jnp.float32)
    up_pre = jnp.einsum("td,efd->etf", all_tokens, w_up, preferred_element_type=jnp.float32)
    sigmoid_gate = jax.nn.sigmoid(gate_pre)
    active = gate_pre * sigmoid_gate
    hidden = (active * up_pre).astype(jnp.bfloat16)
    hidden_grad = jnp.einsum("etd,efd->etf", pair_grads, w_down, preferred_element_type=jnp.float32)
    gate_grad = (
        hidden_grad * up_pre * sigmoid_gate * (1.0 + gate_pre * (1.0 - sigmoid_gate))
    ).astype(jnp.bfloat16)
    up_grad = (hidden_grad * active).astype(jnp.bfloat16)
    back = jnp.einsum(
        "etf,efd->td", gate_grad, w_gate, preferred_element_type=jnp.float32
    ) + jnp.einsum("etf,efd->td", up_grad, w_up, preferred_element_type=jnp.float32)
    shared = lax.psum_scatter(
        back.astype(jnp.bfloat16), "head", scatter_dimension=1, tiled=True
    )
    summed = lax.psum_scatter(shared, "ctx", scatter_dimension=0, tiled=True)
    grad_tokens = lax.all_gather(summed.astype(jnp.bfloat16), "head", axis=1, tiled=True)
    grad_gate = jnp.einsum(
        "etf,td->efd", gate_grad, all_tokens, preferred_element_type=jnp.float32
    ).astype(jnp.bfloat16)
    grad_up = jnp.einsum(
        "etf,td->efd", up_grad, all_tokens, preferred_element_type=jnp.float32
    ).astype(jnp.bfloat16)
    grad_down = jnp.einsum(
        "etf,etd->efd", hidden, pair_grads, preferred_element_type=jnp.float32
    ).astype(jnp.bfloat16)
    return grad_tokens, grad_gate, grad_up, grad_down


def body(
    tokens,
    grad_out,
    expert_ids,
    gate_probs,
    w_gate,
    w_up,
    w_down,
    query_rows,
    key_rows,
    value_rows,
    attn_out,
    grad_attn,
    segment_ids,
):
    tok_count, width = tokens.shape
    top_count = expert_ids.shape[1]
    ctx_count = lax.axis_size("ctx")
    local_experts = w_gate.shape[0]
    total_experts = local_experts * ctx_count
    if tok_count > local_experts * ((5 * tok_count * top_count + 4 * total_experts - 1) // (4 * total_experts)):
        expert_outputs = routed_experts(
            tokens, grad_out, expert_ids, gate_probs, w_gate, w_up, w_down
        )
    else:
        expert_outputs = dense_experts(
            tokens, grad_out, expert_ids, gate_probs, w_gate, w_up, w_down
        )
    grad_tokens, grad_gate, grad_up, grad_down = expert_outputs
    att_rows = query_rows.shape[0]
    kv_width = key_rows.shape[1]
    kv_local = kv_width // HD
    group_size = HQ // KVH
    window = (REACH + 1) * att_rows
    score_scale = HD ** (-0.5)
    ctx_index = lax.axis_index("ctx")
    key_blocks = []
    value_blocks = []
    for distance in range(REACH, 0, -1):
        far_key, far_value = passed_along((key_rows, value_rows), "ctx", distance)
        key_blocks.append(far_key)
        value_blocks.append(far_value)
    window_key = jnp.concatenate(key_blocks + [key_rows], axis=0).reshape(window, kv_local, HD)
    window_value = jnp.concatenate(value_blocks + [value_rows], axis=0).reshape(
        window, kv_local, HD
    )
    query_pos = ctx_index * att_rows + jnp.arange(att_rows, dtype=jnp.int32)
    key_pos = (ctx_index - REACH) * att_rows + jnp.arange(window, dtype=jnp.int32)
    padded_segment = jnp.concatenate([jnp.full((REACH * att_rows,), -1, jnp.int32), segment_ids])
    key_seg = lax.dynamic_slice_in_dim(padded_segment, ctx_index * att_rows, window, 0)
    query_seg = lax.dynamic_slice_in_dim(segment_ids, ctx_index * att_rows, att_rows, 0)
    visible = (key_pos[None, :] <= query_pos[:, None]) & (key_seg[None, :] == query_seg[:, None])
    query_heads = query_rows.reshape(att_rows, kv_local, group_size, HD)
    out_heads = attn_out.reshape(att_rows, kv_local, group_size, HD)
    grad_heads = grad_attn.reshape(att_rows, kv_local, group_size, HD)
    scores = (
        jnp.einsum("ajgd,tjd->jgat", query_heads, window_key, preferred_element_type=jnp.float32)
        * score_scale
    )
    row_peak = jnp.max(jnp.where(visible, scores, -jnp.inf), axis=-1, keepdims=True)
    weights_exp = jnp.exp(jnp.where(visible, scores - row_peak, -jnp.inf))
    probs = weights_exp / jnp.sum(weights_exp, axis=-1, keepdims=True)
    row_delta = jnp.einsum(
        "ajgd,ajgd->jga", grad_heads, out_heads, preferred_element_type=jnp.float32
    )
    prob_grad = jnp.einsum(
        "ajgd,tjd->jgat", grad_heads, window_value, preferred_element_type=jnp.float32
    )
    score_grad = (probs * (prob_grad - row_delta[..., None])).astype(jnp.bfloat16)
    probs_low = probs.astype(jnp.bfloat16)
    grad_query = (
        (
            score_scale
            * jnp.einsum(
                "jgat,tjd->ajgd", score_grad, window_key, preferred_element_type=jnp.float32
            )
        )
        .astype(jnp.bfloat16)
        .reshape(att_rows, -1)
    )
    key_terms = (
        score_scale
        * jnp.einsum("jgat,ajgd->tjd", score_grad, query_heads, preferred_element_type=jnp.float32)
    ).reshape(window, kv_width)
    value_terms = jnp.einsum(
        "jgat,ajgd->tjd", probs_low, grad_heads, preferred_element_type=jnp.float32
    ).reshape(window, kv_width)
    key_total = key_terms[REACH * att_rows :]
    value_total = value_terms[REACH * att_rows :]
    for distance in range(1, REACH + 1):
        offset = (REACH - distance) * att_rows
        got_key, got_value = passed_along(
            (key_terms[offset : offset + att_rows], value_terms[offset : offset + att_rows]),
            "ctx",
            -distance,
        )
        key_total = key_total + got_key
        value_total = value_total + got_value
    return (
        grad_tokens,
        grad_gate,
        grad_up,
        grad_down,
        grad_query,
        key_total.astype(jnp.bfloat16),
        value_total.astype(jnp.bfloat16),
    )


def solution(mesh):
    placed = (
        P("ctx", None),
        P("ctx", None),
        P("ctx", None),
        P("ctx", None),
        P("ctx", "head", None),
        P("ctx", "head", None),
        P("ctx", "head", None),
        P("ctx", "head"),
        P("ctx", "head"),
        P("ctx", "head"),
        P("ctx", "head"),
        P("ctx", "head"),
        P(),
    )
    return jax.shard_map(
        body,
        mesh=mesh,
        in_specs=placed,
        out_specs=(
            P("ctx", None),
            P("ctx", "head", None),
            P("ctx", "head", None),
            P("ctx", "head", None),
            P("ctx", "head"),
            P("ctx", "head"),
            P("ctx", "head"),
        ),
        check_vma=False,
    )
```

```python
import jax
import jax.numpy as jnp
from jax import lax
from jax.experimental import pallas as pl
from jax.experimental.pallas import tpu as pltpu
from jax.sharding import PartitionSpec as P

HQ = 32
KVH = 4
HD = 128
REACH = 3
MESH = pl.DeviceIdType.MESH


def passed_along(block, axis, distance):
    devices = range(lax.axis_size(axis))
    route = [(i - distance, i) for i in devices if i - distance in devices]
    return lax.ppermute(block, axis, route)


def expert_backward(recv_rows, recv_grads, w_gate, w_up, w_down):
    gate_pre = jnp.einsum("secd,efd->secf", recv_rows, w_gate, preferred_element_type=jnp.float32)
    up_pre = jnp.einsum("secd,efd->secf", recv_rows, w_up, preferred_element_type=jnp.float32)
    sigmoid_gate = jax.nn.sigmoid(gate_pre)
    active = gate_pre * sigmoid_gate
    hidden = (active * up_pre).astype(jnp.bfloat16)
    hidden_grad = jnp.einsum(
        "secd,efd->secf", recv_grads, w_down, preferred_element_type=jnp.float32
    )
    gate_grad = (
        hidden_grad * up_pre * sigmoid_gate * (1.0 + gate_pre * (1.0 - sigmoid_gate))
    ).astype(jnp.bfloat16)
    up_grad = (hidden_grad * active).astype(jnp.bfloat16)
    back_rows = jnp.einsum(
        "secf,efd->secd", gate_grad, w_gate, preferred_element_type=jnp.float32
    ) + jnp.einsum("secf,efd->secd", up_grad, w_up, preferred_element_type=jnp.float32)
    grad_gate = jnp.einsum(
        "secf,secd->efd", gate_grad, recv_rows, preferred_element_type=jnp.float32
    ).astype(jnp.bfloat16)
    grad_up = jnp.einsum(
        "secf,secd->efd", up_grad, recv_rows, preferred_element_type=jnp.float32
    ).astype(jnp.bfloat16)
    grad_down = jnp.einsum(
        "secf,secd->efd", hidden, recv_grads, preferred_element_type=jnp.float32
    ).astype(jnp.bfloat16)
    return (back_rows, grad_gate, grad_up, grad_down)


def pair_total(returned, slot_index, tok_count, top_count):
    flat_rows = returned.reshape(-1, returned.shape[3])
    picked = flat_rows[slot_index]
    return jnp.sum(picked.reshape(tok_count, top_count, returned.shape[3]), axis=1)


def routed_experts(tokens, grad_out, expert_ids, gate_probs, w_gate, w_up, w_down):
    tok_count, width = tokens.shape
    top_count = expert_ids.shape[1]
    ctx_count = lax.axis_size("ctx")
    local_experts = w_gate.shape[0]
    total_experts = local_experts * ctx_count
    capacity = (5 * tok_count * top_count + 4 * total_experts - 1) // (4 * total_experts)
    pair_count = tok_count * top_count
    flat_expert = expert_ids.reshape(pair_count)
    onehot = (flat_expert[:, None] == jnp.arange(total_experts, dtype=jnp.int32)[None, :]).astype(
        jnp.int32
    )
    earlier = jnp.cumsum(onehot, axis=0) - onehot
    slot_rank = jnp.sum(earlier * onehot, axis=1)
    slot_index = flat_expert * capacity + slot_rank
    slot_pair = (
        jnp.full((total_experts * capacity,), pair_count, jnp.int32)
        .at[slot_index]
        .set(jnp.arange(pair_count, dtype=jnp.int32))
    )
    slot_token = slot_pair // top_count
    padded_tokens = jnp.concatenate([tokens, jnp.zeros((1, width), tokens.dtype)], axis=0)
    padded_grad = jnp.concatenate([grad_out, jnp.zeros((1, width), grad_out.dtype)], axis=0)
    padded_probs = jnp.concatenate(
        [gate_probs.reshape(pair_count).astype(jnp.float32), jnp.zeros((1,), jnp.float32)]
    )
    buffer_shape = (ctx_count, local_experts, capacity, width)
    send_rows = padded_tokens[slot_token].reshape(buffer_shape)
    send_grads = (
        (padded_probs[slot_pair][:, None] * padded_grad[slot_token].astype(jnp.float32))
        .astype(jnp.bfloat16)
        .reshape(buffer_shape)
    )
    recv_rows, recv_grads = (
        lax.all_to_all(send_rows, "ctx", split_axis=0, concat_axis=0, tiled=True),
        lax.all_to_all(send_grads, "ctx", split_axis=0, concat_axis=0, tiled=True),
    )
    back_rows, grad_gate, grad_up, grad_down = expert_backward(
        recv_rows, recv_grads, w_gate, w_up, w_down
    )
    shared = lax.psum_scatter(back_rows, "head", scatter_dimension=3, tiled=True)
    returned = lax.all_to_all(shared, "ctx", split_axis=0, concat_axis=0, tiled=True)
    summed = pair_total(returned, slot_index, tok_count, top_count)
    grad_tokens = lax.all_gather(summed.astype(jnp.bfloat16), "head", axis=1, tiled=True)
    return grad_tokens, grad_gate, grad_up, grad_down


def dense_experts(tokens, grad_out, expert_ids, gate_probs, w_gate, w_up, w_down):
    ctx_count = lax.axis_size("ctx")
    local_experts = w_gate.shape[0]
    total_experts = local_experts * ctx_count
    chosen = expert_ids[:, :, None] == jnp.arange(total_experts, dtype=jnp.int32)[None, None, :]
    prob_table = jnp.sum(
        jnp.where(chosen, gate_probs.astype(jnp.float32)[:, :, None], 0.0), axis=1
    )
    all_tokens = lax.all_gather(tokens, "ctx", axis=0, tiled=True)
    all_grads = lax.all_gather(grad_out, "ctx", axis=0, tiled=True)
    all_probs = lax.all_gather(prob_table, "ctx", axis=0, tiled=True)
    my_probs = lax.dynamic_slice_in_dim(
        all_probs, lax.axis_index("ctx") * local_experts, local_experts, 1
    )
    pair_grads = (my_probs.T[:, :, None] * all_grads.astype(jnp.float32)[None]).astype(jnp.bfloat16)
    gate_pre = jnp.einsum("td,efd->etf", all_tokens, w_gate, preferred_element_type=jnp.float32)
    up_pre = jnp.einsum("td,efd->etf", all_tokens, w_up, preferred_element_type=jnp.float32)
    sigmoid_gate = jax.nn.sigmoid(gate_pre)
    active = gate_pre * sigmoid_gate
    hidden = (active * up_pre).astype(jnp.bfloat16)
    hidden_grad = jnp.einsum("etd,efd->etf", pair_grads, w_down, preferred_element_type=jnp.float32)
    gate_grad = (
        hidden_grad * up_pre * sigmoid_gate * (1.0 + gate_pre * (1.0 - sigmoid_gate))
    ).astype(jnp.bfloat16)
    up_grad = (hidden_grad * active).astype(jnp.bfloat16)
    back = jnp.einsum(
        "etf,efd->td", gate_grad, w_gate, preferred_element_type=jnp.float32
    ) + jnp.einsum("etf,efd->td", up_grad, w_up, preferred_element_type=jnp.float32)
    shared = lax.psum_scatter(
        back.astype(jnp.bfloat16), "head", scatter_dimension=1, tiled=True
    )
    summed = lax.psum_scatter(shared, "ctx", scatter_dimension=0, tiled=True)
    grad_tokens = lax.all_gather(summed.astype(jnp.bfloat16), "head", axis=1, tiled=True)
    grad_gate = jnp.einsum(
        "etf,td->efd", gate_grad, all_tokens, preferred_element_type=jnp.float32
    ).astype(jnp.bfloat16)
    grad_up = jnp.einsum(
        "etf,td->efd", up_grad, all_tokens, preferred_element_type=jnp.float32
    ).astype(jnp.bfloat16)
    grad_down = jnp.einsum(
        "etf,etd->efd", hidden, pair_grads, preferred_element_type=jnp.float32
    ).astype(jnp.bfloat16)
    return grad_tokens, grad_gate, grad_up, grad_down


def body(
    tokens,
    grad_out,
    expert_ids,
    gate_probs,
    w_gate,
    w_up,
    w_down,
    query_rows,
    key_rows,
    value_rows,
    attn_out,
    grad_attn,
    segment_ids,
):
    tok_count, width = tokens.shape
    top_count = expert_ids.shape[1]
    ctx_count = lax.axis_size("ctx")
    local_experts = w_gate.shape[0]
    total_experts = local_experts * ctx_count
    if tok_count > local_experts * ((5 * tok_count * top_count + 4 * total_experts - 1) // (4 * total_experts)):
        expert_outputs = routed_experts(
            tokens, grad_out, expert_ids, gate_probs, w_gate, w_up, w_down
        )
    else:
        expert_outputs = dense_experts(
            tokens, grad_out, expert_ids, gate_probs, w_gate, w_up, w_down
        )
    grad_tokens, grad_gate, grad_up, grad_down = expert_outputs
    att_rows = query_rows.shape[0]
    kv_width = key_rows.shape[1]
    kv_local = kv_width // HD
    group_size = HQ // KVH
    window = (REACH + 1) * att_rows
    score_scale = HD ** (-0.5)
    ctx_index = lax.axis_index("ctx")
    key_blocks = []
    value_blocks = []
    for distance in range(REACH, 0, -1):
        far_key, far_value = passed_along((key_rows, value_rows), "ctx", distance)
        key_blocks.append(far_key)
        value_blocks.append(far_value)
    window_key = jnp.concatenate(key_blocks + [key_rows], axis=0).reshape(window, kv_local, HD)
    window_value = jnp.concatenate(value_blocks + [value_rows], axis=0).reshape(
        window, kv_local, HD
    )
    query_pos = ctx_index * att_rows + jnp.arange(att_rows, dtype=jnp.int32)
    key_pos = (ctx_index - REACH) * att_rows + jnp.arange(window, dtype=jnp.int32)
    padded_segment = jnp.concatenate([jnp.full((REACH * att_rows,), -1, jnp.int32), segment_ids])
    key_seg = lax.dynamic_slice_in_dim(padded_segment, ctx_index * att_rows, window, 0)
    query_seg = lax.dynamic_slice_in_dim(segment_ids, ctx_index * att_rows, att_rows, 0)
    visible = (key_pos[None, :] <= query_pos[:, None]) & (key_seg[None, :] == query_seg[:, None])
    query_heads = query_rows.reshape(att_rows, kv_local, group_size, HD)
    out_heads = attn_out.reshape(att_rows, kv_local, group_size, HD)
    grad_heads = grad_attn.reshape(att_rows, kv_local, group_size, HD)
    scores = (
        jnp.einsum("ajgd,tjd->jgat", query_heads, window_key, preferred_element_type=jnp.float32)
        * score_scale
    )
    row_peak = jnp.max(jnp.where(visible, scores, -jnp.inf), axis=-1, keepdims=True)
    weights_exp = jnp.exp(jnp.where(visible, scores - row_peak, -jnp.inf))
    probs = weights_exp / jnp.sum(weights_exp, axis=-1, keepdims=True)
    row_delta = jnp.einsum(
        "ajgd,ajgd->jga", grad_heads, out_heads, preferred_element_type=jnp.float32
    )
    prob_grad = jnp.einsum(
        "ajgd,tjd->jgat", grad_heads, window_value, preferred_element_type=jnp.float32
    )
    score_grad = (probs * (prob_grad - row_delta[..., None])).astype(jnp.bfloat16)
    probs_low = probs.astype(jnp.bfloat16)
    grad_query = (
        (
            score_scale
            * jnp.einsum(
                "jgat,tjd->ajgd", score_grad, window_key, preferred_element_type=jnp.float32
            )
        )
        .astype(jnp.bfloat16)
        .reshape(att_rows, -1)
    )
    key_terms = (
        score_scale
        * jnp.einsum("jgat,ajgd->tjd", score_grad, query_heads, preferred_element_type=jnp.float32)
    ).reshape(window, kv_width)
    value_terms = jnp.einsum(
        "jgat,ajgd->tjd", probs_low, grad_heads, preferred_element_type=jnp.float32
    ).reshape(window, kv_width)
    key_total = key_terms[REACH * att_rows :]
    value_total = value_terms[REACH * att_rows :]
    for distance in range(1, REACH + 1):
        offset = (REACH - distance) * att_rows
        got_key, got_value = passed_along(
            (key_terms[offset : offset + att_rows], value_terms[offset : offset + att_rows]),
            "ctx",
            -distance,
        )
        key_total = key_total + got_key
        value_total = value_total + got_value
    return (
        grad_tokens,
        grad_gate,
        grad_up,
        grad_down,
        grad_query,
        key_total.astype(jnp.bfloat16),
        value_total.astype(jnp.bfloat16),
    )


def combined_kernel(
    tok, grd, side_in, wg, wu, wd, q_in, o_in, ga_in, vis,
    gtok_o, gg_o, gu_o, gd_o, dq_o, dk_o, dv_o,
    g, side, ggs, ugs, hds, send_c, recv_c, acc, send_y, recv_y, send_x, recv_x,
    send_z, recv_z, total, fin, sgs, pls, qs, gas, kv_own, kv_send, kv_recv,
    zs, zr, ys, yr, xs, xr, cs, cr, rcs, rcr, rys, ryr, rxs, rxr, rzs, rzr, fs, fr, ks, kr,
):
    f32, bf16 = jnp.float32, jnp.bfloat16
    rows, quarter = g.shape[3], g.shape[4]
    ctx, head = lax.axis_index("ctx"), lax.axis_index("head")
    z, y = ctx // 2, ctx % 2
    x, c = head // 2, head % 2
    head_x = (1 - x) * 2 + c
    head_c = x * 2 + (1 - c)
    head_xc = (1 - x) * 2 + (1 - c)
    ctx_y = z * 2 + (1 - y)
    upper = z // 2
    near = upper * (3 - z) + (1 - upper) * z
    order = [upper * (3 - f) + (1 - upper) * f for f in (near, 1 - near, 2, 3)]
    order = [jnp.int32(v) if isinstance(v, int) else v for v in order]

    def remote(src, dst, send_sem, recv_sem, to_ctx, to_head):
        return pltpu.make_async_remote_copy(
            src_ref=src, dst_ref=dst, send_sem=send_sem, recv_sem=recv_sem,
            device_id=(to_ctx, to_head), device_id_type=MESH,
        )

    pending = []

    def send(copy, condition=None):
        if condition is None:
            copy.start()
        else:
            pl.when(condition)(copy.start)
        pending.append((copy, condition))

    barrier = pltpu.get_barrier_semaphore()

    def greet(to_ctx, to_head):
        pl.semaphore_signal(barrier, inc=1, device_id=(to_ctx, to_head), device_id_type=MESH)

    for other in (head_x, head_c):
        greet(ctx, other)
    for away in range(1, 8):
        greet((ctx + away) % 8, head)

    def own_quarter(q):
        cols = pl.ds(pl.multiple_of(q * quarter, quarter), quarter)
        g[0, q, ctx] = tok[:, cols]
        g[1, q, ctx] = grd[:, cols]

    own_quarter(head)
    side[ctx] = side_in[...]
    pl.semaphore_wait(barrier, 9)

    def piece(q, b):
        return g.at[:, q, b]

    def send_z_dir(zp, slot, to_z):
        b = zp * 2 + y
        there = (to_z >= 0) & (to_z < 4)
        to_ctx = to_z * 2 + y
        send(remote(piece(head, b), piece(head, b), zs.at[0, slot], zr.at[0, zp], to_ctx, head), there)
        send(remote(side.at[b], side.at[b], zs.at[1, slot], zr.at[1, zp], to_ctx, head), there)

    def send_y_dir(i):
        b = order[i] * 2 + y
        send(remote(piece(head, b), piece(head, b), ys.at[0, i], yr.at[0, i], ctx_y, head))
        send(remote(side.at[b], side.at[b], ys.at[1, i], yr.at[1, i], ctx_y, head))

    blocks = {}
    for k, (kind, i) in enumerate(("B0", "A1", "B1", "A2", "B2", "A3", "B3")):
        i = int(i)
        blocks[kind + str(i)] = (k, order[i] * 2 + (y if kind == "A" else 1 - y))

    def send_x_dir(name):
        k, b = blocks[name]
        send(remote(piece(head, b), piece(head, b), xs.at[k], xr.at[k], ctx, head_x))
        send(remote(piece(head, b), piece(head, b), cs.at[k, 0], cr.at[k, 0], ctx, head_c))

    def got_z(i):
        zp = order[i]
        b = zp * 2 + y
        remote(piece(head, b), piece(head, b), zs.at[0, i], zr.at[0, zp], ctx, head).wait_recv()
        remote(side.at[b], side.at[b], zs.at[1, i], zr.at[1, zp], ctx, head).wait_recv()
        below = jnp.where(zp < z, 1, -1)
        send_z_dir(zp, i + 1, z + below)
        send_y_dir(i)

    def got_y(i):
        b = order[i] * 2 + (1 - y)
        remote(piece(head, b), piece(head, b), ys.at[0, i], yr.at[0, i], ctx, head).wait_recv()
        remote(side.at[b], side.at[b], ys.at[1, i], yr.at[1, i], ctx, head).wait_recv()

    def got_x(name):
        k, b = blocks[name]
        part = piece(head_x, b)
        remote(part, part, xs.at[k], xr.at[k], ctx, head).wait_recv()
        send(remote(part, part, cs.at[k, 1], cr.at[k, 1], ctx, head_c))

    def got_c(name):
        k, b = blocks[name]
        for at, q in ((0, head_c), (1, head_xc)):
            part = piece(q, b)
            remote(part, part, cs.at[k, at], cr.at[k, at], ctx, head).wait_recv()

    def nt(a, b):
        return lax.dot_general(a, b, (((1,), (1,)), ((), ())), preferred_element_type=f32)

    def tn(a, b):
        return lax.dot_general(a, b, (((0,), (0,)), ((), ())), preferred_element_type=f32)

    units = wg.shape[0] // 2

    def pair_compute(i):
        zp = order[i]
        pair = pl.ds(zp * 2, 2)
        gate_pre = up_pre = hid = None
        for q in range(4):
            cols = slice(q * quarter, (q + 1) * quarter)
            t = g[0, q, pair].reshape(2 * rows, quarter)
            d = g[1, q, pair].reshape(2 * rows, quarter)
            parts = (nt(t, wg[:, cols]), nt(t, wu[:, cols]), nt(d, wd[:, cols]))
            if q == 0:
                gate_pre, up_pre, hid = parts
            else:
                gate_pre, up_pre, hid = gate_pre + parts[0], up_pre + parts[1], hid + parts[2]
        table = side[pair, :, 0:128].reshape(2 * rows, 128).astype(f32)
        lane = lax.broadcasted_iota(jnp.int32, (2 * rows, 128), 1)
        p0 = jnp.sum(jnp.where(lane == 2 * ctx, table, 0.0), axis=1, keepdims=True)
        p1 = jnp.sum(jnp.where(lane == 2 * ctx + 1, table, 0.0), axis=1, keepdims=True)
        unit = lax.broadcasted_iota(jnp.int32, (2 * rows, 2 * units), 1)
        prob = jnp.where(unit < units, p0, p1)
        hid = hid * prob
        s = jax.nn.sigmoid(gate_pre)
        active = gate_pre * s
        gate_grad = (hid * up_pre * s * (1.0 + gate_pre * (1.0 - s))).astype(bf16)
        up_grad = (hid * active).astype(bf16)
        ggs[zp] = gate_grad
        ugs[zp] = up_grad
        hds[zp] = (active * up_pre * prob).astype(bf16)

        def back(q):
            cols = pl.ds(pl.multiple_of(q * quarter, quarter), quarter)
            return jnp.dot(gate_grad, wg[:, cols], preferred_element_type=f32) + jnp.dot(
                up_grad, wu[:, cols], preferred_element_type=f32
            )

        for xx in range(2):
            send_c[i, xx] = back(2 * xx + (1 - c)).astype(bf16)
        send(remote(send_c.at[i], recv_c.at[i], rcs.at[i], rcr.at[i], ctx, head_c))
        for xx in range(2):
            acc[i, xx] = back(2 * xx + c).reshape(2, rows, quarter)

    def return_y(i):
        remote(send_c.at[i], recv_c.at[i], rcs.at[i], rcr.at[i], ctx, head).wait_recv()
        for xx in range(2):
            send_y[i, xx] = (
                acc[i, xx, 1 - y] + recv_c[i, xx, pl.ds((1 - y) * rows, rows)].astype(f32)
            ).astype(bf16)
        send(remote(send_y.at[i], recv_y.at[i], rys.at[i], ryr.at[i], ctx_y, head))

    def return_x(i):
        remote(send_y.at[i], recv_y.at[i], rys.at[i], ryr.at[i], ctx, head).wait_recv()

        def mine(xx):
            return (
                acc[i, xx, y]
                + recv_c[i, xx, pl.ds(y * rows, rows)].astype(f32)
                + recv_y[i, xx].astype(f32)
            )

        send_x[i] = mine(1 - x).astype(bf16)
        send(remote(send_x.at[i], recv_x.at[i], rxs.at[i], rxr.at[i], ctx, head_x))
        total[i] = mine(x)

    def return_z(i):
        remote(send_x.at[i], recv_x.at[i], rxs.at[i], rxr.at[i], ctx, head).wait_recv()
        value = total[i] + recv_x[i].astype(f32)
        if i == 0:
            total[i] = value
        else:
            send_z[i] = value.astype(bf16)
            send(remote(
                send_z.at[i], recv_z.at[z], rzs.at[i], rzr.at[z], order[i] * 2 + y, head
            ))

    scale = HD ** (-0.5)
    heads = q_in.shape[1] // HD

    def attention():
        starts = [jnp.maximum(ctx - j, 0) for j in (3, 2, 1, 0)]
        key = jnp.concatenate([side[b, :, 128:256] for b in starts], axis=0)
        value = jnp.concatenate([side[b, :, 256:384] for b in starts], axis=0)
        seen = vis[...] > 0
        for h in range(heads):
            cols = slice(h * HD, (h + 1) * HD)
            at = slice(h * rows, (h + 1) * rows)
            qh, gh = q_in[:, cols], ga_in[:, cols]
            qs[at, :] = qh
            gas[at, :] = gh
            scores = jnp.where(seen, nt(qh, key) * scale, -jnp.inf)
            peak = jnp.max(scores, axis=1, keepdims=True)
            weight = jnp.exp(scores - peak)
            probs = weight / jnp.sum(weight, axis=1, keepdims=True)
            delta = jnp.sum(
                gh.astype(f32) * o_in[:, cols].astype(f32), axis=1, keepdims=True
            )
            sg = (probs * (nt(gh, value) - delta)).astype(bf16)
            sgs[at, :] = sg
            pls[at, :] = probs.astype(bf16)
            dq_o[:, cols] = (
                scale * jnp.dot(sg, key, preferred_element_type=f32)
            ).astype(bf16)
        key_terms = scale * tn(sgs[...], qs[...])
        value_terms = tn(pls[...], gas[...])
        for j in (1, 2, 3):
            at = slice((3 - j) * rows, (4 - j) * rows)
            kv_send[j - 1, :, 0:HD] = key_terms[at]
            kv_send[j - 1, :, HD : 2 * HD] = value_terms[at]
            send(
                remote(kv_send.at[j - 1], kv_recv.at[j - 1], ks.at[j - 1], kr.at[j - 1], ctx - j, head),
                ctx - j >= 0,
            )
        kv_own[:, 0:HD] = key_terms[3 * rows :]
        kv_own[:, HD : 2 * HD] = value_terms[3 * rows :]

    def attention_end():
        for j in (1, 2, 3):

            @pl.when(ctx + j < 8)
            def _():
                remote(
                    kv_send.at[j - 1], kv_recv.at[j - 1], ks.at[j - 1], kr.at[j - 1], ctx, head
                ).wait_recv()
                kv_own[...] += kv_recv[j - 1]

        dk_o[...] = kv_own[:, 0:HD].astype(bf16)
        dv_o[...] = kv_own[:, HD : 2 * HD].astype(bf16)

    def weight_grad(source, which, out):
        flat = source[...].reshape(8 * rows, 2 * units)
        for q in range(4):
            cols = slice(q * quarter, (q + 1) * quarter)
            out[:, cols] = tn(flat, g[which, q].reshape(8 * rows, quarter)).astype(bf16)

    send_z_dir(z, 0, z + 1)
    send_z_dir(z, 1, z - 1)
    send_y_dir(0)
    for away in (1, 2, 3):
        own_quarter((head + away) % 4)
    got_y(0)
    send_x_dir("B0")
    got_z(1)
    send_x_dir("A1")
    got_z(2)
    got_y(1)
    send_x_dir("B1")
    send_x_dir("A2")
    got_x("B0")
    got_c("B0")
    pair_compute(0)
    got_z(3)
    got_y(2)
    send_x_dir("B2")
    send_x_dir("A3")
    got_y(3)
    send_x_dir("B3")
    got_x("A1")
    return_y(0)
    attention()
    for name in ("B1", "A2"):
        got_x(name)
    got_c("A1")
    got_c("B1")
    pair_compute(1)
    return_x(0)
    got_x("B2")
    got_c("A2")
    got_c("B2")
    return_y(1)
    pair_compute(2)
    return_z(0)
    return_x(1)
    got_x("A3")
    got_x("B3")
    got_c("A3")
    got_c("B3")
    return_y(2)
    pair_compute(3)
    return_z(1)
    return_x(2)
    weight_grad(ggs, 0, gg_o)
    return_y(3)
    return_z(2)
    attention_end()
    return_x(3)
    weight_grad(ugs, 0, gu_o)
    return_z(3)
    weight_grad(hds, 1, gd_o)
    result = total[0]
    for j in (1, 2, 3):
        other = (z + j) % 4
        remote(send_z.at[j], recv_z.at[other], rzs.at[j], rzr.at[other], ctx, head).wait_recv()
        result = result + recv_z[other].astype(f32)
    fin[head] = result.astype(bf16)
    send(remote(fin.at[head], fin.at[head], fs.at[0], fr.at[0], ctx, head_x))
    send(remote(fin.at[head], fin.at[head], fs.at[1], fr.at[1], ctx, head_c))
    remote(fin.at[head_x], fin.at[head_x], fs.at[0], fr.at[0], ctx, head).wait_recv()
    send(remote(fin.at[head_x], fin.at[head_x], fs.at[2], fr.at[2], ctx, head_c))
    remote(fin.at[head_c], fin.at[head_c], fs.at[1], fr.at[1], ctx, head).wait_recv()
    remote(fin.at[head_xc], fin.at[head_xc], fs.at[2], fr.at[2], ctx, head).wait_recv()
    for q in range(4):
        gtok_o[:, q * quarter : (q + 1) * quarter] = fin[q]
    for copy, condition in pending:
        if condition is None:
            copy.wait_send()
        else:
            pl.when(condition)(copy.wait_send)


def combined_body(
    tokens, grad_out, expert_ids, gate_probs, w_gate, w_up, w_down,
    query_rows, key_rows, value_rows, attn_out, grad_attn, segment_ids,
):
    rows, width = tokens.shape
    local_experts, units, _ = w_gate.shape
    quarter = width // 4
    f32, bf16 = jnp.float32, jnp.bfloat16
    chosen = expert_ids[:, :, None] == jnp.arange(128, dtype=jnp.int32)[None, None, :]
    table = jnp.sum(jnp.where(chosen, gate_probs.astype(f32)[:, :, None], 0.0), axis=1).astype(bf16)
    side_rows = jnp.concatenate([table, key_rows, value_rows], axis=1)
    window = (REACH + 1) * rows
    ctx_index = lax.axis_index("ctx")
    query_pos = ctx_index * rows + jnp.arange(rows, dtype=jnp.int32)
    key_pos = (ctx_index - REACH) * rows + jnp.arange(window, dtype=jnp.int32)
    padded_segment = jnp.concatenate([jnp.full((REACH * rows,), -1, jnp.int32), segment_ids])
    key_seg = lax.dynamic_slice_in_dim(padded_segment, ctx_index * rows, window, 0)
    query_seg = lax.dynamic_slice_in_dim(segment_ids, ctx_index * rows, rows, 0)
    visible = (
        (key_pos[None, :] <= query_pos[:, None]) & (key_seg[None, :] == query_seg[:, None])
    ).astype(f32)
    both = local_experts * units
    flat = [w.reshape(both, width) for w in (w_gate, w_up, w_down)]
    vmem = pl.BlockSpec(memory_space=pltpu.VMEM)
    dma = pltpu.SemaphoreType.DMA
    att_width = query_rows.shape[1]
    shapes = [
        (rows, width), (both, width), (both, width), (both, width),
        (rows, att_width), (rows, HD), (rows, HD),
    ]
    stacked = rows * (att_width // HD)
    outs = pl.pallas_call(
        combined_kernel,
        out_shape=[jax.ShapeDtypeStruct(s, bf16) for s in shapes],
        in_specs=[vmem] * 10,
        out_specs=[vmem] * 7,
        scratch_shapes=[
            pltpu.VMEM((2, 4, 8, rows, quarter), bf16),
            pltpu.VMEM((8, rows, 384), bf16),
            pltpu.VMEM((4, 2 * rows, both), bf16),
            pltpu.VMEM((4, 2 * rows, both), bf16),
            pltpu.VMEM((4, 2 * rows, both), bf16),
            pltpu.VMEM((4, 2, 2 * rows, quarter), bf16),
            pltpu.VMEM((4, 2, 2 * rows, quarter), bf16),
            pltpu.VMEM((4, 2, 2, rows, quarter), f32),
            pltpu.VMEM((4, 2, rows, quarter), bf16),
            pltpu.VMEM((4, 2, rows, quarter), bf16),
            pltpu.VMEM((4, rows, quarter), bf16),
            pltpu.VMEM((4, rows, quarter), bf16),
            pltpu.VMEM((4, rows, quarter), bf16),
            pltpu.VMEM((4, rows, quarter), bf16),
            pltpu.VMEM((4, rows, quarter), f32),
            pltpu.VMEM((4, rows, quarter), bf16),
            pltpu.VMEM((stacked, window), bf16),
            pltpu.VMEM((stacked, window), bf16),
            pltpu.VMEM((stacked, HD), bf16),
            pltpu.VMEM((stacked, HD), bf16),
            pltpu.VMEM((rows, 2 * HD), f32),
            pltpu.VMEM((3, rows, 2 * HD), f32),
            pltpu.VMEM((3, rows, 2 * HD), f32),
            dma((2, 5)), dma((2, 4)), dma((2, 4)), dma((2, 4)),
            dma((7,)), dma((7,)), dma((7, 2)), dma((7, 2)),
            dma((4,)), dma((4,)), dma((4,)), dma((4,)), dma((4,)), dma((4,)),
            dma((4,)), dma((4,)), dma((3,)), dma((3,)), dma((3,)), dma((3,)),
        ],
        compiler_params=pltpu.CompilerParams(
            collective_id=0, has_side_effects=True, vmem_limit_bytes=58 * 1024 * 1024
        ),
        cost_estimate=pl.CostEstimate(
            flops=8 * 2 * 8 * rows * width * both, bytes_accessed=6 * both * width * 2,
            transcendentals=0,
        ),
    )(tokens, grad_out, side_rows, *flat, query_rows, attn_out, grad_attn, visible)
    grads = [w.reshape(local_experts, units, width) for w in outs[1:4]]
    return (outs[0], *grads, *outs[4:])


def chosen_body(*blocks):
    tokens, expert_ids, w_gate, query_rows = blocks[0], blocks[2], blocks[4], blocks[7]
    ctx_count, head_count = lax.axis_size("ctx"), lax.axis_size("head")
    pairs = 5 * tokens.shape[0] * expert_ids.shape[1]
    slots = w_gate.shape[0] * -(-pairs // (4 * w_gate.shape[0] * ctx_count))
    fits = ctx_count == 8 and head_count == 4 and w_gate.shape[0] == 2
    same_rows = tokens.shape[0] == query_rows.shape[0] and blocks[8].shape[1] == HD
    if fits and same_rows and slots >= tokens.shape[0]:
        return combined_body(*blocks)
    return body(*blocks)


def solution(mesh):
    placed = (
        P("ctx", None),
        P("ctx", None),
        P("ctx", None),
        P("ctx", None),
        P("ctx", "head", None),
        P("ctx", "head", None),
        P("ctx", "head", None),
        P("ctx", "head"),
        P("ctx", "head"),
        P("ctx", "head"),
        P("ctx", "head"),
        P("ctx", "head"),
        P(),
    )
    return jax.shard_map(
        chosen_body,
        mesh=mesh,
        in_specs=placed,
        out_specs=(
            P("ctx", None),
            P("ctx", "head", None),
            P("ctx", "head", None),
            P("ctx", "head", None),
            P("ctx", "head"),
            P("ctx", "head"),
            P("ctx", "head"),
        ),
        check_vma=False,
    )
```

```python
import jax
import jax.numpy as jnp
from jax import lax
from jax.experimental import pallas as pl
from jax.experimental.pallas import tpu as pltpu
from jax.sharding import PartitionSpec as P

HQ = 32
KVH = 4
HD = 128
REACH = 3
MESH = pl.DeviceIdType.MESH


def passed_along(block, axis, distance):
    devices = range(lax.axis_size(axis))
    route = [(i - distance, i) for i in devices if i - distance in devices]
    return lax.ppermute(block, axis, route)


def expert_backward(recv_rows, recv_grads, w_gate, w_up, w_down):
    gate_pre = jnp.einsum("secd,efd->secf", recv_rows, w_gate, preferred_element_type=jnp.float32)
    up_pre = jnp.einsum("secd,efd->secf", recv_rows, w_up, preferred_element_type=jnp.float32)
    sigmoid_gate = jax.nn.sigmoid(gate_pre)
    active = gate_pre * sigmoid_gate
    hidden = (active * up_pre).astype(jnp.bfloat16)
    hidden_grad = jnp.einsum(
        "secd,efd->secf", recv_grads, w_down, preferred_element_type=jnp.float32
    )
    gate_grad = (
        hidden_grad * up_pre * sigmoid_gate * (1.0 + gate_pre * (1.0 - sigmoid_gate))
    ).astype(jnp.bfloat16)
    up_grad = (hidden_grad * active).astype(jnp.bfloat16)
    back_rows = jnp.einsum(
        "secf,efd->secd", gate_grad, w_gate, preferred_element_type=jnp.float32
    ) + jnp.einsum("secf,efd->secd", up_grad, w_up, preferred_element_type=jnp.float32)
    grad_gate = jnp.einsum(
        "secf,secd->efd", gate_grad, recv_rows, preferred_element_type=jnp.float32
    ).astype(jnp.bfloat16)
    grad_up = jnp.einsum(
        "secf,secd->efd", up_grad, recv_rows, preferred_element_type=jnp.float32
    ).astype(jnp.bfloat16)
    grad_down = jnp.einsum(
        "secf,secd->efd", hidden, recv_grads, preferred_element_type=jnp.float32
    ).astype(jnp.bfloat16)
    return (back_rows, grad_gate, grad_up, grad_down)


def pair_total(returned, slot_index, tok_count, top_count):
    flat_rows = returned.reshape(-1, returned.shape[3])
    picked = flat_rows[slot_index]
    return jnp.sum(picked.reshape(tok_count, top_count, returned.shape[3]), axis=1)


def routed_experts(tokens, grad_out, expert_ids, gate_probs, w_gate, w_up, w_down):
    tok_count, width = tokens.shape
    top_count = expert_ids.shape[1]
    ctx_count = lax.axis_size("ctx")
    local_experts = w_gate.shape[0]
    total_experts = local_experts * ctx_count
    capacity = (5 * tok_count * top_count + 4 * total_experts - 1) // (4 * total_experts)
    pair_count = tok_count * top_count
    flat_expert = expert_ids.reshape(pair_count)
    onehot = (flat_expert[:, None] == jnp.arange(total_experts, dtype=jnp.int32)[None, :]).astype(
        jnp.int32
    )
    earlier = jnp.cumsum(onehot, axis=0) - onehot
    slot_rank = jnp.sum(earlier * onehot, axis=1)
    slot_index = flat_expert * capacity + slot_rank
    slot_pair = (
        jnp.full((total_experts * capacity,), pair_count, jnp.int32)
        .at[slot_index]
        .set(jnp.arange(pair_count, dtype=jnp.int32))
    )
    slot_token = slot_pair // top_count
    padded_tokens = jnp.concatenate([tokens, jnp.zeros((1, width), tokens.dtype)], axis=0)
    padded_grad = jnp.concatenate([grad_out, jnp.zeros((1, width), grad_out.dtype)], axis=0)
    padded_probs = jnp.concatenate(
        [gate_probs.reshape(pair_count).astype(jnp.float32), jnp.zeros((1,), jnp.float32)]
    )
    buffer_shape = (ctx_count, local_experts, capacity, width)
    send_rows = padded_tokens[slot_token].reshape(buffer_shape)
    send_grads = (
        (padded_probs[slot_pair][:, None] * padded_grad[slot_token].astype(jnp.float32))
        .astype(jnp.bfloat16)
        .reshape(buffer_shape)
    )
    recv_rows, recv_grads = (
        lax.all_to_all(send_rows, "ctx", split_axis=0, concat_axis=0, tiled=True),
        lax.all_to_all(send_grads, "ctx", split_axis=0, concat_axis=0, tiled=True),
    )
    back_rows, grad_gate, grad_up, grad_down = expert_backward(
        recv_rows, recv_grads, w_gate, w_up, w_down
    )
    shared = lax.psum_scatter(back_rows, "head", scatter_dimension=3, tiled=True)
    returned = lax.all_to_all(shared, "ctx", split_axis=0, concat_axis=0, tiled=True)
    summed = pair_total(returned, slot_index, tok_count, top_count)
    grad_tokens = lax.all_gather(summed.astype(jnp.bfloat16), "head", axis=1, tiled=True)
    return grad_tokens, grad_gate, grad_up, grad_down


def dense_experts(tokens, grad_out, expert_ids, gate_probs, w_gate, w_up, w_down):
    ctx_count = lax.axis_size("ctx")
    local_experts = w_gate.shape[0]
    total_experts = local_experts * ctx_count
    chosen = expert_ids[:, :, None] == jnp.arange(total_experts, dtype=jnp.int32)[None, None, :]
    prob_table = jnp.sum(
        jnp.where(chosen, gate_probs.astype(jnp.float32)[:, :, None], 0.0), axis=1
    )
    all_tokens = lax.all_gather(tokens, "ctx", axis=0, tiled=True)
    all_grads = lax.all_gather(grad_out, "ctx", axis=0, tiled=True)
    all_probs = lax.all_gather(prob_table, "ctx", axis=0, tiled=True)
    my_probs = lax.dynamic_slice_in_dim(
        all_probs, lax.axis_index("ctx") * local_experts, local_experts, 1
    )
    pair_grads = (my_probs.T[:, :, None] * all_grads.astype(jnp.float32)[None]).astype(jnp.bfloat16)
    gate_pre = jnp.einsum("td,efd->etf", all_tokens, w_gate, preferred_element_type=jnp.float32)
    up_pre = jnp.einsum("td,efd->etf", all_tokens, w_up, preferred_element_type=jnp.float32)
    sigmoid_gate = jax.nn.sigmoid(gate_pre)
    active = gate_pre * sigmoid_gate
    hidden = (active * up_pre).astype(jnp.bfloat16)
    hidden_grad = jnp.einsum("etd,efd->etf", pair_grads, w_down, preferred_element_type=jnp.float32)
    gate_grad = (
        hidden_grad * up_pre * sigmoid_gate * (1.0 + gate_pre * (1.0 - sigmoid_gate))
    ).astype(jnp.bfloat16)
    up_grad = (hidden_grad * active).astype(jnp.bfloat16)
    back = jnp.einsum(
        "etf,efd->td", gate_grad, w_gate, preferred_element_type=jnp.float32
    ) + jnp.einsum("etf,efd->td", up_grad, w_up, preferred_element_type=jnp.float32)
    shared = lax.psum_scatter(
        back.astype(jnp.bfloat16), "head", scatter_dimension=1, tiled=True
    )
    summed = lax.psum_scatter(shared, "ctx", scatter_dimension=0, tiled=True)
    grad_tokens = lax.all_gather(summed.astype(jnp.bfloat16), "head", axis=1, tiled=True)
    grad_gate = jnp.einsum(
        "etf,td->efd", gate_grad, all_tokens, preferred_element_type=jnp.float32
    ).astype(jnp.bfloat16)
    grad_up = jnp.einsum(
        "etf,td->efd", up_grad, all_tokens, preferred_element_type=jnp.float32
    ).astype(jnp.bfloat16)
    grad_down = jnp.einsum(
        "etf,etd->efd", hidden, pair_grads, preferred_element_type=jnp.float32
    ).astype(jnp.bfloat16)
    return grad_tokens, grad_gate, grad_up, grad_down


def body(
    tokens,
    grad_out,
    expert_ids,
    gate_probs,
    w_gate,
    w_up,
    w_down,
    query_rows,
    key_rows,
    value_rows,
    attn_out,
    grad_attn,
    segment_ids,
):
    tok_count, width = tokens.shape
    top_count = expert_ids.shape[1]
    ctx_count = lax.axis_size("ctx")
    local_experts = w_gate.shape[0]
    total_experts = local_experts * ctx_count
    if tok_count > local_experts * ((5 * tok_count * top_count + 4 * total_experts - 1) // (4 * total_experts)):
        expert_outputs = routed_experts(
            tokens, grad_out, expert_ids, gate_probs, w_gate, w_up, w_down
        )
    else:
        expert_outputs = dense_experts(
            tokens, grad_out, expert_ids, gate_probs, w_gate, w_up, w_down
        )
    grad_tokens, grad_gate, grad_up, grad_down = expert_outputs
    att_rows = query_rows.shape[0]
    kv_width = key_rows.shape[1]
    kv_local = kv_width // HD
    group_size = HQ // KVH
    window = (REACH + 1) * att_rows
    score_scale = HD ** (-0.5)
    ctx_index = lax.axis_index("ctx")
    key_blocks = []
    value_blocks = []
    for distance in range(REACH, 0, -1):
        far_key, far_value = passed_along((key_rows, value_rows), "ctx", distance)
        key_blocks.append(far_key)
        value_blocks.append(far_value)
    window_key = jnp.concatenate(key_blocks + [key_rows], axis=0).reshape(window, kv_local, HD)
    window_value = jnp.concatenate(value_blocks + [value_rows], axis=0).reshape(
        window, kv_local, HD
    )
    query_pos = ctx_index * att_rows + jnp.arange(att_rows, dtype=jnp.int32)
    key_pos = (ctx_index - REACH) * att_rows + jnp.arange(window, dtype=jnp.int32)
    padded_segment = jnp.concatenate([jnp.full((REACH * att_rows,), -1, jnp.int32), segment_ids])
    key_seg = lax.dynamic_slice_in_dim(padded_segment, ctx_index * att_rows, window, 0)
    query_seg = lax.dynamic_slice_in_dim(segment_ids, ctx_index * att_rows, att_rows, 0)
    visible = (key_pos[None, :] <= query_pos[:, None]) & (key_seg[None, :] == query_seg[:, None])
    query_heads = query_rows.reshape(att_rows, kv_local, group_size, HD)
    out_heads = attn_out.reshape(att_rows, kv_local, group_size, HD)
    grad_heads = grad_attn.reshape(att_rows, kv_local, group_size, HD)
    scores = (
        jnp.einsum("ajgd,tjd->jgat", query_heads, window_key, preferred_element_type=jnp.float32)
        * score_scale
    )
    row_peak = jnp.max(jnp.where(visible, scores, -jnp.inf), axis=-1, keepdims=True)
    weights_exp = jnp.exp(jnp.where(visible, scores - row_peak, -jnp.inf))
    probs = weights_exp / jnp.sum(weights_exp, axis=-1, keepdims=True)
    row_delta = jnp.einsum(
        "ajgd,ajgd->jga", grad_heads, out_heads, preferred_element_type=jnp.float32
    )
    prob_grad = jnp.einsum(
        "ajgd,tjd->jgat", grad_heads, window_value, preferred_element_type=jnp.float32
    )
    score_grad = (probs * (prob_grad - row_delta[..., None])).astype(jnp.bfloat16)
    probs_low = probs.astype(jnp.bfloat16)
    grad_query = (
        (
            score_scale
            * jnp.einsum(
                "jgat,tjd->ajgd", score_grad, window_key, preferred_element_type=jnp.float32
            )
        )
        .astype(jnp.bfloat16)
        .reshape(att_rows, -1)
    )
    key_terms = (
        score_scale
        * jnp.einsum("jgat,ajgd->tjd", score_grad, query_heads, preferred_element_type=jnp.float32)
    ).reshape(window, kv_width)
    value_terms = jnp.einsum(
        "jgat,ajgd->tjd", probs_low, grad_heads, preferred_element_type=jnp.float32
    ).reshape(window, kv_width)
    key_total = key_terms[REACH * att_rows :]
    value_total = value_terms[REACH * att_rows :]
    for distance in range(1, REACH + 1):
        offset = (REACH - distance) * att_rows
        got_key, got_value = passed_along(
            (key_terms[offset : offset + att_rows], value_terms[offset : offset + att_rows]),
            "ctx",
            -distance,
        )
        key_total = key_total + got_key
        value_total = value_total + got_value
    return (
        grad_tokens,
        grad_gate,
        grad_up,
        grad_down,
        grad_query,
        key_total.astype(jnp.bfloat16),
        value_total.astype(jnp.bfloat16),
    )


def combined_kernel(
    tok, grd, side_in, wg, wu, wd, q_in, o_in, ga_in, vis,
    gtok_o, gg_o, gu_o, gd_o, dq_o, dk_o, dv_o,
    g, side, ggs, ugs, hds, send_c, recv_c, acc, send_y, recv_y, send_x, recv_x,
    send_z, recv_z, total, fin, sgs, pls, qs, gas, kv_own, kv_send, kv_recv, wacc,
    zs, zr, ys, yr, xs, xr, cs, cr, rcs, rcr, rys, ryr, rxs, rxr, rzs, rzr, fs, fr, ks, kr,
):
    f32, bf16 = jnp.float32, jnp.bfloat16
    rows, quarter = g.shape[3], g.shape[4]
    ctx, head = lax.axis_index("ctx"), lax.axis_index("head")
    z, y = ctx // 2, ctx % 2
    x, c = head // 2, head % 2
    head_x = (1 - x) * 2 + c
    head_c = x * 2 + (1 - c)
    head_xc = (1 - x) * 2 + (1 - c)
    ctx_y = z * 2 + (1 - y)
    upper = z // 2
    near = upper * (3 - z) + (1 - upper) * z
    order = [upper * (3 - f) + (1 - upper) * f for f in (near, 1 - near, 2, 3)]
    order = [jnp.int32(v) if isinstance(v, int) else v for v in order]

    def remote(src, dst, send_sem, recv_sem, to_ctx, to_head):
        return pltpu.make_async_remote_copy(
            src_ref=src, dst_ref=dst, send_sem=send_sem, recv_sem=recv_sem,
            device_id=(to_ctx, to_head), device_id_type=MESH,
        )

    pending = []

    def send(copy, condition=None):
        if condition is None:
            copy.start()
        else:
            pl.when(condition)(copy.start)
        pending.append((copy, condition))

    barrier = pltpu.get_barrier_semaphore()

    def greet(to_ctx, to_head):
        pl.semaphore_signal(barrier, inc=1, device_id=(to_ctx, to_head), device_id_type=MESH)

    for other in (head_x, head_c):
        greet(ctx, other)
    for away in range(1, 8):
        greet((ctx + away) % 8, head)

    def own_quarter(q):
        cols = pl.ds(pl.multiple_of(q * quarter, quarter), quarter)
        g[0, q, ctx] = tok[:, cols]
        g[1, q, ctx] = grd[:, cols]

    own_quarter(head)
    side[ctx] = side_in[...]
    pl.semaphore_wait(barrier, 9)

    def piece(q, b):
        return g.at[:, q, b]

    def send_z_dir(zp, slot, to_z):
        b = zp * 2 + y
        there = (to_z >= 0) & (to_z < 4)
        to_ctx = to_z * 2 + y
        send(remote(piece(head, b), piece(head, b), zs.at[0, slot], zr.at[0, zp], to_ctx, head), there)
        send(remote(side.at[b], side.at[b], zs.at[1, slot], zr.at[1, zp], to_ctx, head), there)

    def send_y_dir(i):
        b = order[i] * 2 + y
        send(remote(piece(head, b), piece(head, b), ys.at[0, i], yr.at[0, i], ctx_y, head))
        send(remote(side.at[b], side.at[b], ys.at[1, i], yr.at[1, i], ctx_y, head))

    blocks = {}
    for k, (kind, i) in enumerate(("B0", "A1", "B1", "A2", "B2", "A3", "B3")):
        i = int(i)
        blocks[kind + str(i)] = (k, order[i] * 2 + (y if kind == "A" else 1 - y))

    def send_x_dir(name):
        k, b = blocks[name]
        send(remote(piece(head, b), piece(head, b), xs.at[k], xr.at[k], ctx, head_x))
        send(remote(piece(head, b), piece(head, b), cs.at[k, 0], cr.at[k, 0], ctx, head_c))

    def got_z(i):
        zp = order[i]
        b = zp * 2 + y
        remote(piece(head, b), piece(head, b), zs.at[0, i], zr.at[0, zp], ctx, head).wait_recv()
        remote(side.at[b], side.at[b], zs.at[1, i], zr.at[1, zp], ctx, head).wait_recv()
        below = jnp.where(zp < z, 1, -1)
        send_z_dir(zp, i + 1, z + below)
        send_y_dir(i)

    def got_y(i):
        b = order[i] * 2 + (1 - y)
        remote(piece(head, b), piece(head, b), ys.at[0, i], yr.at[0, i], ctx, head).wait_recv()
        remote(side.at[b], side.at[b], ys.at[1, i], yr.at[1, i], ctx, head).wait_recv()

    def got_x(name):
        k, b = blocks[name]
        part = piece(head_x, b)
        remote(part, part, xs.at[k], xr.at[k], ctx, head).wait_recv()
        send(remote(part, part, cs.at[k, 1], cr.at[k, 1], ctx, head_c))

    def got_c(name):
        k, b = blocks[name]
        for at, q in ((0, head_c), (1, head_xc)):
            part = piece(q, b)
            remote(part, part, cs.at[k, at], cr.at[k, at], ctx, head).wait_recv()

    def nt(a, b):
        return lax.dot_general(a, b, (((1,), (1,)), ((), ())), preferred_element_type=f32)

    def tn(a, b):
        return lax.dot_general(a, b, (((0,), (0,)), ((), ())), preferred_element_type=f32)

    units = wg.shape[0] // 2

    def pair_compute(i):
        zp = order[i]
        pair = pl.ds(zp * 2, 2)
        gate_pre = up_pre = hid = None
        for q in range(4):
            cols = slice(q * quarter, (q + 1) * quarter)
            t = g[0, q, pair].reshape(2 * rows, quarter)
            d = g[1, q, pair].reshape(2 * rows, quarter)
            parts = (nt(t, wg[:, cols]), nt(t, wu[:, cols]), nt(d, wd[:, cols]))
            if q == 0:
                gate_pre, up_pre, hid = parts
            else:
                gate_pre, up_pre, hid = gate_pre + parts[0], up_pre + parts[1], hid + parts[2]
        table = side[pair, :, 0:128].reshape(2 * rows, 128).astype(f32)
        lane = lax.broadcasted_iota(jnp.int32, (2 * rows, 128), 1)
        p0 = jnp.sum(jnp.where(lane == 2 * ctx, table, 0.0), axis=1, keepdims=True)
        p1 = jnp.sum(jnp.where(lane == 2 * ctx + 1, table, 0.0), axis=1, keepdims=True)
        unit = lax.broadcasted_iota(jnp.int32, (2 * rows, 2 * units), 1)
        prob = jnp.where(unit < units, p0, p1)
        hid = hid * prob
        s = jax.nn.sigmoid(gate_pre)
        active = gate_pre * s
        gate_grad = (hid * up_pre * s * (1.0 + gate_pre * (1.0 - s))).astype(bf16)
        up_grad = (hid * active).astype(bf16)
        ggs[zp] = gate_grad
        ugs[zp] = up_grad
        hds[zp] = (active * up_pre * prob).astype(bf16)

        def back(q):
            cols = pl.ds(pl.multiple_of(q * quarter, quarter), quarter)
            return jnp.dot(gate_grad, wg[:, cols], preferred_element_type=f32) + jnp.dot(
                up_grad, wu[:, cols], preferred_element_type=f32
            )

        for xx in range(2):
            send_c[i, xx] = back(2 * xx + (1 - c)).astype(bf16)
        send(remote(send_c.at[i], recv_c.at[i], rcs.at[i], rcr.at[i], ctx, head_c))
        for xx in range(2):
            acc[i, xx] = back(2 * xx + c).reshape(2, rows, quarter)

    def return_y(i):
        remote(send_c.at[i], recv_c.at[i], rcs.at[i], rcr.at[i], ctx, head).wait_recv()
        for xx in range(2):
            send_y[i, xx] = (
                acc[i, xx, 1 - y] + recv_c[i, xx, pl.ds((1 - y) * rows, rows)].astype(f32)
            ).astype(bf16)
        send(remote(send_y.at[i], recv_y.at[i], rys.at[i], ryr.at[i], ctx_y, head))

    def return_x(i):
        remote(send_y.at[i], recv_y.at[i], rys.at[i], ryr.at[i], ctx, head).wait_recv()

        def mine(xx):
            return (
                acc[i, xx, y]
                + recv_c[i, xx, pl.ds(y * rows, rows)].astype(f32)
                + recv_y[i, xx].astype(f32)
            )

        send_x[i] = mine(1 - x).astype(bf16)
        send(remote(send_x.at[i], recv_x.at[i], rxs.at[i], rxr.at[i], ctx, head_x))
        total[i] = mine(x)

    def return_z(i):
        remote(send_x.at[i], recv_x.at[i], rxs.at[i], rxr.at[i], ctx, head).wait_recv()
        value = total[i] + recv_x[i].astype(f32)
        if i == 0:
            total[i] = value
        else:
            send_z[i] = value.astype(bf16)
            send(remote(
                send_z.at[i], recv_z.at[z], rzs.at[i], rzr.at[z], order[i] * 2 + y, head
            ))

    scale = HD ** (-0.5)
    heads = q_in.shape[1] // HD

    def attention():
        starts = [jnp.maximum(ctx - j, 0) for j in (3, 2, 1, 0)]
        key = jnp.concatenate([side[b, :, 128:256] for b in starts], axis=0)
        value = jnp.concatenate([side[b, :, 256:384] for b in starts], axis=0)
        seen = vis[...] > 0
        for h in range(heads):
            cols = slice(h * HD, (h + 1) * HD)
            at = slice(h * rows, (h + 1) * rows)
            qh, gh = q_in[:, cols], ga_in[:, cols]
            qs[at, :] = qh
            gas[at, :] = gh
            scores = jnp.where(seen, nt(qh, key) * scale, -jnp.inf)
            peak = jnp.max(scores, axis=1, keepdims=True)
            weight = jnp.exp(scores - peak)
            probs = weight / jnp.sum(weight, axis=1, keepdims=True)
            delta = jnp.sum(
                gh.astype(f32) * o_in[:, cols].astype(f32), axis=1, keepdims=True
            )
            sg = (probs * (nt(gh, value) - delta)).astype(bf16)
            sgs[at, :] = sg
            pls[at, :] = probs.astype(bf16)
            dq_o[:, cols] = (
                scale * jnp.dot(sg, key, preferred_element_type=f32)
            ).astype(bf16)
        key_terms = scale * tn(sgs[...], qs[...])
        value_terms = tn(pls[...], gas[...])
        for j in (1, 2, 3):
            at = slice((3 - j) * rows, (4 - j) * rows)
            kv_send[j - 1, :, 0:HD] = key_terms[at]
            kv_send[j - 1, :, HD : 2 * HD] = value_terms[at]
            send(
                remote(kv_send.at[j - 1], kv_recv.at[j - 1], ks.at[j - 1], kr.at[j - 1], ctx - j, head),
                ctx - j >= 0,
            )
        kv_own[:, 0:HD] = key_terms[3 * rows :]
        kv_own[:, HD : 2 * HD] = value_terms[3 * rows :]

    def attention_end():
        for j in (1, 2, 3):

            @pl.when(ctx + j < 8)
            def _():
                remote(
                    kv_send.at[j - 1], kv_recv.at[j - 1], ks.at[j - 1], kr.at[j - 1], ctx, head
                ).wait_recv()
                kv_own[...] += kv_recv[j - 1]

        dk_o[...] = kv_own[:, 0:HD].astype(bf16)
        dv_o[...] = kv_own[:, HD : 2 * HD].astype(bf16)

    def half_terms(source, which, q, half):
        flat = source[pl.ds(2 * half, 2)].reshape(4 * rows, 2 * units)
        return tn(flat, g[which, q, pl.ds(4 * half, 4)].reshape(4 * rows, quarter))

    def first_half(source, which, at):
        for q in range(4):
            wacc[at, :, q * quarter : (q + 1) * quarter] = half_terms(source, which, q, upper)

    def weight_grad(source, which, at, out):
        for q in range(4):
            cols = slice(q * quarter, (q + 1) * quarter)
            out[:, cols] = (
                wacc[at, :, cols] + half_terms(source, which, q, 1 - upper)
            ).astype(bf16)

    send_z_dir(z, 0, z + 1)
    send_z_dir(z, 1, z - 1)
    send_y_dir(0)
    for away in (1, 2, 3):
        own_quarter((head + away) % 4)
    got_y(0)
    send_x_dir("B0")
    got_z(1)
    send_x_dir("A1")
    got_z(2)
    got_y(1)
    send_x_dir("B1")
    send_x_dir("A2")
    got_x("B0")
    got_c("B0")
    pair_compute(0)
    got_z(3)
    got_y(2)
    send_x_dir("B2")
    send_x_dir("A3")
    got_y(3)
    send_x_dir("B3")
    got_x("A1")
    return_y(0)
    attention()
    for name in ("B1", "A2"):
        got_x(name)
    got_c("A1")
    got_c("B1")
    pair_compute(1)
    return_x(0)
    first_half(ggs, 0, 0)
    got_x("B2")
    got_c("A2")
    got_c("B2")
    return_y(1)
    pair_compute(2)
    return_z(0)
    return_x(1)
    first_half(ugs, 0, 1)
    got_x("A3")
    first_half(hds, 1, 2)
    got_x("B3")
    got_c("A3")
    got_c("B3")
    return_y(2)
    pair_compute(3)
    return_z(1)
    return_x(2)
    weight_grad(ggs, 0, 0, gg_o)
    return_y(3)
    return_z(2)
    attention_end()
    return_x(3)
    weight_grad(ugs, 0, 1, gu_o)
    return_z(3)
    weight_grad(hds, 1, 2, gd_o)
    result = total[0]
    for j in (1, 2, 3):
        other = (z + j) % 4
        remote(send_z.at[j], recv_z.at[other], rzs.at[j], rzr.at[other], ctx, head).wait_recv()
        result = result + recv_z[other].astype(f32)
    fin[head] = result.astype(bf16)
    send(remote(fin.at[head], fin.at[head], fs.at[0], fr.at[0], ctx, head_x))
    send(remote(fin.at[head], fin.at[head], fs.at[1], fr.at[1], ctx, head_c))
    remote(fin.at[head_x], fin.at[head_x], fs.at[0], fr.at[0], ctx, head).wait_recv()
    send(remote(fin.at[head_x], fin.at[head_x], fs.at[2], fr.at[2], ctx, head_c))
    remote(fin.at[head_c], fin.at[head_c], fs.at[1], fr.at[1], ctx, head).wait_recv()
    remote(fin.at[head_xc], fin.at[head_xc], fs.at[2], fr.at[2], ctx, head).wait_recv()
    for q in range(4):
        gtok_o[:, q * quarter : (q + 1) * quarter] = fin[q]
    for copy, condition in pending:
        if condition is None:
            copy.wait_send()
        else:
            pl.when(condition)(copy.wait_send)


def combined_body(
    tokens, grad_out, expert_ids, gate_probs, w_gate, w_up, w_down,
    query_rows, key_rows, value_rows, attn_out, grad_attn, segment_ids,
):
    rows, width = tokens.shape
    local_experts, units, _ = w_gate.shape
    quarter = width // 4
    f32, bf16 = jnp.float32, jnp.bfloat16
    chosen = expert_ids[:, :, None] == jnp.arange(128, dtype=jnp.int32)[None, None, :]
    table = jnp.sum(jnp.where(chosen, gate_probs.astype(f32)[:, :, None], 0.0), axis=1).astype(bf16)
    side_rows = jnp.concatenate([table, key_rows, value_rows], axis=1)
    window = (REACH + 1) * rows
    ctx_index = lax.axis_index("ctx")
    query_pos = ctx_index * rows + jnp.arange(rows, dtype=jnp.int32)
    key_pos = (ctx_index - REACH) * rows + jnp.arange(window, dtype=jnp.int32)
    padded_segment = jnp.concatenate([jnp.full((REACH * rows,), -1, jnp.int32), segment_ids])
    key_seg = lax.dynamic_slice_in_dim(padded_segment, ctx_index * rows, window, 0)
    query_seg = lax.dynamic_slice_in_dim(segment_ids, ctx_index * rows, rows, 0)
    visible = (
        (key_pos[None, :] <= query_pos[:, None]) & (key_seg[None, :] == query_seg[:, None])
    ).astype(f32)
    both = local_experts * units
    flat = [w.reshape(both, width) for w in (w_gate, w_up, w_down)]
    vmem = pl.BlockSpec(memory_space=pltpu.VMEM)
    dma = pltpu.SemaphoreType.DMA
    att_width = query_rows.shape[1]
    shapes = [
        (rows, width), (both, width), (both, width), (both, width),
        (rows, att_width), (rows, HD), (rows, HD),
    ]
    stacked = rows * (att_width // HD)
    outs = pl.pallas_call(
        combined_kernel,
        out_shape=[jax.ShapeDtypeStruct(s, bf16) for s in shapes],
        in_specs=[vmem] * 10,
        out_specs=[vmem] * 7,
        scratch_shapes=[
            pltpu.VMEM((2, 4, 8, rows, quarter), bf16),
            pltpu.VMEM((8, rows, 384), bf16),
            pltpu.VMEM((4, 2 * rows, both), bf16),
            pltpu.VMEM((4, 2 * rows, both), bf16),
            pltpu.VMEM((4, 2 * rows, both), bf16),
            pltpu.VMEM((4, 2, 2 * rows, quarter), bf16),
            pltpu.VMEM((4, 2, 2 * rows, quarter), bf16),
            pltpu.VMEM((4, 2, 2, rows, quarter), f32),
            pltpu.VMEM((4, 2, rows, quarter), bf16),
            pltpu.VMEM((4, 2, rows, quarter), bf16),
            pltpu.VMEM((4, rows, quarter), bf16),
            pltpu.VMEM((4, rows, quarter), bf16),
            pltpu.VMEM((4, rows, quarter), bf16),
            pltpu.VMEM((4, rows, quarter), bf16),
            pltpu.VMEM((4, rows, quarter), f32),
            pltpu.VMEM((4, rows, quarter), bf16),
            pltpu.VMEM((stacked, window), bf16),
            pltpu.VMEM((stacked, window), bf16),
            pltpu.VMEM((stacked, HD), bf16),
            pltpu.VMEM((stacked, HD), bf16),
            pltpu.VMEM((rows, 2 * HD), f32),
            pltpu.VMEM((3, rows, 2 * HD), f32),
            pltpu.VMEM((3, rows, 2 * HD), f32),
            pltpu.VMEM((3, both, width), f32),
            dma((2, 5)), dma((2, 4)), dma((2, 4)), dma((2, 4)),
            dma((7,)), dma((7,)), dma((7, 2)), dma((7, 2)),
            dma((4,)), dma((4,)), dma((4,)), dma((4,)), dma((4,)), dma((4,)),
            dma((4,)), dma((4,)), dma((3,)), dma((3,)), dma((3,)), dma((3,)),
        ],
        compiler_params=pltpu.CompilerParams(
            collective_id=0, has_side_effects=True, vmem_limit_bytes=58 * 1024 * 1024
        ),
        cost_estimate=pl.CostEstimate(
            flops=8 * 2 * 8 * rows * width * both, bytes_accessed=6 * both * width * 2,
            transcendentals=0,
        ),
    )(tokens, grad_out, side_rows, *flat, query_rows, attn_out, grad_attn, visible)
    grads = [w.reshape(local_experts, units, width) for w in outs[1:4]]
    return (outs[0], *grads, *outs[4:])


def chosen_body(*blocks):
    tokens, expert_ids, w_gate, query_rows = blocks[0], blocks[2], blocks[4], blocks[7]
    ctx_count, head_count = lax.axis_size("ctx"), lax.axis_size("head")
    pairs = 5 * tokens.shape[0] * expert_ids.shape[1]
    slots = w_gate.shape[0] * -(-pairs // (4 * w_gate.shape[0] * ctx_count))
    fits = ctx_count == 8 and head_count == 4 and w_gate.shape[0] == 2
    same_rows = tokens.shape[0] == query_rows.shape[0] and blocks[8].shape[1] == HD
    if fits and same_rows and slots >= tokens.shape[0]:
        return combined_body(*blocks)
    return body(*blocks)


def solution(mesh):
    placed = (
        P("ctx", None),
        P("ctx", None),
        P("ctx", None),
        P("ctx", None),
        P("ctx", "head", None),
        P("ctx", "head", None),
        P("ctx", "head", None),
        P("ctx", "head"),
        P("ctx", "head"),
        P("ctx", "head"),
        P("ctx", "head"),
        P("ctx", "head"),
        P(),
    )
    return jax.shard_map(
        chosen_body,
        mesh=mesh,
        in_specs=placed,
        out_specs=(
            P("ctx", None),
            P("ctx", "head", None),
            P("ctx", "head", None),
            P("ctx", "head", None),
            P("ctx", "head"),
            P("ctx", "head"),
            P("ctx", "head"),
        ),
        check_vma=False,
    )
```
